512 devices in a mesh: dp: 8 (over y), expert: 64 (over x, z, core).
Axes of the slice: x: 4, y: 8, z: 8, core: 2. Of those that a mesh axis runs over, the one named last changes fastest.
Arguments:
- hidden_in: bfloat16 [16384, 2880], P('expert', 'dp'), may hold values from -70 to 70
- norm_gain: float32 [2880], P('dp'), may hold values from 0.25 to 1.75
- expert_ids: int32 [16384, 4], P('expert'), may hold values from 0 to 63, all different within a row; in each aligned block of 256 rows (0 to 255, 256 to 511, ...) at most 24 rows name the same one
- route_weights: float32 [16384, 4], P('expert'), may hold values from 0.1 to 0.5
- gate_weight: bfloat16 [64, 1440, 2880], P('expert', 'dp'), may hold values from -0.109375 to 0.109375
- up_weight: bfloat16 [64, 1440, 2880], P('expert', 'dp'), may hold values from -0.109375 to 0.109375
- down_weight: bfloat16 [64, 1440, 2880], P('expert', None, 'dp'), may hold values from -0.15625 to 0.15625
Outputs:
- expert_out: bfloat16 [16384, 2880], P('expert', 'dp')
- peaks: float32 [16384], P('expert')
The draws below stay inside these ranges and needn't reach their ends.
Inputs may be any that keep to these rules, and one draw needn't show every extreme that they name: `expert_ids`: the 4 experts of a token differ. Among the 256 tokens of one index of expert, no expert is named more than 24 times, a bound that some block reaches.
All inputs are finite; a program needn't handle non-finite values.
Results may differ from the reference program's by a relative error of at most 0.025.
Values may be sent and summed in bfloat16 or wider, within the bound.
A program may use at most 64 MiB of HBM per device.

```python
import math
import jax
import jax.numpy as jnp
import numpy as np
from jax import lax

D = 2880
FF = 1440
TOP = 4
TOK_DEV = 256
TOKENS = 16384
EXPERTS = 64
CAP = 24
N_EXPERT = 64


def draw_hidden_in(key, part):
    key = jax.random.fold_in(key, 1)
    base_key, row_key, col_key = jax.random.split(key, 3)
    row_level = 10.0 ** jax.random.uniform(row_key, (TOKENS, 1), jnp.float32, -0.5, 0.5)
    trend = 3.0 ** (jnp.arange(D, dtype=jnp.float32) / D - 0.5)
    col_level = 10.0 ** jax.random.uniform(col_key, (1, D), jnp.float32, -0.5, 0.5) * trend[None, :]
    base = jnp.clip(jax.random.normal(base_key, (TOKENS, D)), -4.0, 4.0)
    return (base * row_level * col_level).astype(jnp.bfloat16)


def level_of(stream_key, shape, shards, smallest, largest):
    level = 1.0
    for axis_at, blocks in shards:
        steps = jax.random.uniform(jax.random.fold_in(jax.random.fold_in(stream_key, 6), axis_at), (blocks,), jnp.float32, smallest / len(shards), largest / len(shards))
        level = level * jnp.repeat(jnp.exp(steps), shape[axis_at] // blocks).reshape((-1,) + (1,) * (len(shape) - 1 - axis_at))
    return level


def assign_block(stream_key, own, number, rows, count, top, bound, lean):
    sequence = jax.random.permutation(stream_key, count)
    packed, ordinary = portions_of(count, rows * top, bound, lean, True), portions_of(count, rows * top, bound, lean, False)
    places = jnp.arange(count)

    def named(lengths, turn):
        used = int((lengths > 0).sum())
        fixed = max(1, used // 4)
        shifted = fixed + (places - fixed + turn * (used - fixed)) % max(1, count - fixed)
        return jnp.zeros((count,), jnp.int32).at[sequence[jnp.where(places < fixed, places, shifted)]].set(jnp.asarray(lengths, jnp.int32))

    lengths = jnp.where(number % 4 == 0, named(packed, number // 4), named(ordinary, number - number // 4 - 1))
    mixed = jax.random.permutation(jax.random.fold_in(own, 3), count)
    donor, receiver = mixed[0:count // 2 * 2:2], mixed[1:count // 2 * 2:2]
    margin = jnp.minimum(lengths[donor] - 1, bound - lengths[receiver]) // 2
    margin = jnp.where((donor == sequence[0]) | (receiver == sequence[0]) | (lengths[receiver] == 0), 0, jnp.maximum(margin, 0))
    shifted = jax.random.randint(jax.random.fold_in(own, 4), (count // 2,), 0, 1 << 20) % (margin + 1)
    lengths = lengths.at[donor].add(-shifted).at[receiver].add(shifted)
    items = jnp.searchsorted(jnp.cumsum(lengths), jnp.arange(rows * top), side="right").astype(jnp.int32)
    table = items.reshape(top, rows).T
    table = table[jax.random.permutation(jax.random.fold_in(own, 1), rows)]
    turn = jax.random.randint(jax.random.fold_in(own, 2), (rows, 1), 0, top)
    return jnp.take_along_axis(table, (jnp.arange(top)[None, :] + turn) % top, axis=1)


def portions_of(count, total, reach, slope, full):
    loads = [(1 << 20) // math.isqrt(grade ** slope) + 1 for grade in range(1, count + 1)]
    largest = reach if full else min(reach, max(-(-total // count), total * loads[0] // sum(loads)))
    least = 1 if total - largest >= count - 1 else 0
    given, surplus = [largest] + [least] * (count - 1), total - largest - least * (count - 1)
    while surplus > 0:
        candidates = [i for i in range(1, count) if given[i] < largest] or [i for i in range(1, count) if given[i] < reach]
        mass, budget = sum([loads[i] for i in candidates]), surplus
        for i in candidates:
            extra = min(reach - given[i], max(1, budget * loads[i] // mass), surplus)
            given[i] = given[i] + extra
            surplus = surplus - extra
    return np.array(given)


def normal_values(own_key, extent, scale, limit, cuts=(), kind=jnp.bfloat16):
    entries = scale * jax.random.normal(own_key, extent, jnp.float32)
    if cuts:
        entries = entries * level_of(own_key, extent, cuts, -0.22, 0.18)
    return jnp.clip(entries, -limit, limit).astype(kind)


def setup_inputs(seed: int = 0) -> dict:
    keys = jax.random.split(jax.random.key(seed), 8)
    hidden_in = draw_hidden_in(jax.random.fold_in(keys[7], 71), 0)
    norm_gain = jnp.clip(1.0 + 0.15 * jax.random.normal(keys[1], (D,), jnp.float32), 0.25, 1.75)
    expert_ids_keys = jax.random.split(jax.random.fold_in(keys[2], 1), TOKENS // TOK_DEV)
    expert_ids_turns = jax.random.permutation(jax.random.fold_in(keys[2], 3), TOKENS // TOK_DEV)
    expert_ids = jax.vmap(lambda own, number: assign_block(jax.random.fold_in(keys[2], 2), own, number, TOK_DEV, EXPERTS, TOP, CAP, 2))(expert_ids_keys, expert_ids_turns).reshape((TOKENS, TOP))
    route_weights = jnp.clip(0.1 + 0.4 * jax.random.uniform(keys[3], (TOKENS, TOP), jnp.float32) ** level_of(keys[3], (TOKENS, TOP), ((0, 64),), -0.2, 0.2), 0.1, 0.5)
    gate_weight = normal_values(keys[4], (EXPERTS, FF, D), D ** -0.5, 0.109375, ((0, 64), (1, 8)))
    up_weight = normal_values(keys[5], (EXPERTS, FF, D), D ** -0.5, 0.109375, ((0, 64), (1, 8)))
    down_weight = normal_values(keys[6], (EXPERTS, FF, D), FF ** -0.5, 0.15625, ((0, 64), (2, 8)))
    return {"hidden_in": hidden_in, "norm_gain": norm_gain, "expert_ids": expert_ids, "route_weights": route_weights, "gate_weight": gate_weight, "up_weight": up_weight, "down_weight": down_weight}


def reference(hidden_in, norm_gain, expert_ids, route_weights, gate_weight, up_weight, down_weight):
    widened = hidden_in.astype(jnp.float32)
    totals = lax.optimization_barrier(jnp.sum(widened * widened, axis=1))
    inverse = lax.rsqrt(totals / D + 1e-05)
    normed = widened * inverse[:, None] * norm_gain
    peaks = lax.optimization_barrier(jnp.max(jnp.abs(normed), axis=1))
    token_scale = ((peaks + 1e-06) / 448.0).astype(jnp.bfloat16)
    payload = (normed / token_scale.astype(jnp.float32)[:, None]).astype(jnp.bfloat16)
    flat_ids = expert_ids.reshape(-1)
    pair_count = TOKENS * TOP
    slot_total = N_EXPERT * CAP
    padded_rows = jnp.concatenate([payload, jnp.zeros((1, D), jnp.bfloat16)], axis=0)
    padded_scale = jnp.concatenate([token_scale.astype(jnp.float32), jnp.zeros((1,), jnp.float32)])
    padded_weight = jnp.concatenate([route_weights.reshape(-1), jnp.zeros((1,), jnp.float32)])

    def one_expert(running, bundle):
        gate_part, up_part, down_part, number = bundle
        chosen = jnp.nonzero(flat_ids == number, size=slot_total, fill_value=pair_count)[0].astype(jnp.int32)
        source_row = (chosen // TOP).astype(jnp.int32)
        row_block = padded_rows[source_row]
        row_scale = padded_scale[source_row][:, None]
        gate_val = row_scale * jnp.dot(row_block, gate_part.T, preferred_element_type=jnp.float32)
        up_val = row_scale * jnp.dot(row_block, up_part.T, preferred_element_type=jnp.float32)
        hidden = (gate_val * jax.nn.sigmoid(1.702 * gate_val) * (up_val + 1.0)).astype(jnp.bfloat16)
        expert_rows = jnp.dot(hidden, down_part, preferred_element_type=jnp.float32).astype(jnp.bfloat16)
        weighted = padded_weight[chosen][:, None] * expert_rows.astype(jnp.float32)
        running = running.at[source_row].add(weighted, mode='drop')
        return (running, None)
    running, unused = lax.scan(one_expert, jnp.zeros((TOKENS, D), jnp.float32), (gate_weight, up_weight, down_weight, jnp.arange(EXPERTS, dtype=jnp.int32)))
    expert_out = running.astype(jnp.bfloat16)
    return (expert_out, peaks)
```

```python
import jax
import jax.numpy as jnp
from jax import lax
from jax.experimental import pallas as pl
from jax.experimental.pallas import tpu as pltpu
from jax.sharding import PartitionSpec as P

D = 2880
TOP = 4
CAP = 24
MESH = pl.DeviceIdType.MESH
F32 = jnp.float32
BF16 = jnp.bfloat16

NY = 8
NX, NZ, NC = 4, 8, 2
NE = NX * NZ * NC
PARTS = NX * NC
REL = NZ
ROWS = REL * CAP
HALF = ROWS // 2
TOK = 256
FEAT = D // NY
UNITS = 180
LANES = 384
TAIL = 64
TALL = 320
SUM_ROW = TAIL + 184
NT = (((1,), (1,)), ((), ()))


def kernel(
    hid_ref, gain_ref, ids_ref, rw_ref, gate_ref, up_ref, down_ref,
    out_ref, peaks_ref,
    xs, key_s, wsel_s, pwt_s, send_s, gx, gh, wg_s, wu_s, wd_s, ret_out, ret_in, stats_s,
    acc_g, acc_u, acc_o, acc_t,
    pre_send, pre_recv, disp_send, disp_recv, x_send_s, x_recv_s, h_send_s, h_recv_s,
    ret_send, ret_recv, st_send, st_recv,
):
    my_y = lax.axis_index("dp")
    my_e = lax.axis_index("expert")
    my_x = my_e // (NZ * NC)
    my_z = (my_e // NC) % NZ
    my_c = my_e % NC
    right = (my_y + 1) % NY
    left = (my_y + NY - 1) % NY

    barrier = pltpu.get_barrier_semaphore()

    @pl.loop(1, NE)
    def _(i):
        pl.semaphore_signal(
            barrier, inc=1, device_id=(my_y, (my_e + i) % NE), device_id_type=MESH
        )

    @pl.loop(1, NY)
    def _(i):
        pl.semaphore_signal(
            barrier, inc=1, device_id=((my_y + i) % NY, my_e), device_id_type=MESH
        )

    hid = hid_ref[...].astype(F32)
    scaled = hid * gain_ref[...]
    total = jnp.sum(hid * hid, axis=1, keepdims=True)
    high = total.astype(BF16).astype(F32)
    low = total - high
    xs[1, :, 0:FEAT] = scaled.astype(BF16)
    last = xs[1, :, 256:LANES].astype(F32)
    lane = lax.broadcasted_iota(jnp.int32, (TOK, 128), 1)
    at = FEAT - 256
    last = jnp.where(lane < at, last, 0.0)
    last = jnp.where(lane == at, high, last)
    last = jnp.where(lane == at + 1, low, last)
    xs[1, :, 256:LANES] = last.astype(BF16)
    biggest = jnp.max(jnp.abs(scaled), axis=1, keepdims=True)
    pair = jnp.where(lane == 0, total, jnp.where(lane == 1, biggest, 0.0))
    stats_s[0] = pair.T[0:8, :]

    named = jnp.zeros((TOK, 128), F32)
    weight = jnp.zeros((TOK, 128), F32)
    for j in range(TOP):
        hit = ids_ref[:, j : j + 1] == lane
        named = jnp.where(hit, 1.0, named)
        weight = jnp.where(hit, rw_ref[:, j : j + 1], weight)
    named_t = named.T[0:NE, :]
    wsel_s[...] = weight.T[0:NE, :]
    earlier = (
        lax.broadcasted_iota(jnp.int32, (TOK, TOK), 0)
        < lax.broadcasted_iota(jnp.int32, (TOK, TOK), 1)
    )
    earlier = jnp.where(earlier, 1.0, 0.0).astype(BF16)
    before = jnp.dot(named_t.astype(BF16), earlier, preferred_element_type=F32)
    key_s[...] = jnp.where(named_t > 0.5, before, -1.0)

    def place(part, j, sign):
        dx, dc = part // NC, part % NC
        x = (my_x + NX + sign * dx) % NX
        z = (my_z + NZ + sign * j) % NZ
        c = (my_c + dc) % NC
        return (x * NZ + z) * NC + c

    rank = lax.broadcasted_iota(jnp.int32, (CAP, TOK), 0).astype(F32)

    def selection(part):
        picks, weighted = [], []
        for j in range(REL):
            e = place(part, j, 1)
            hit = key_s[pl.ds(e, 1), :] == rank
            picks.append(jnp.where(hit, 1.0, 0.0))
            weighted.append(jnp.where(hit, wsel_s[pl.ds(e, 1), :], 0.0))
        weighted = jnp.concatenate(weighted, axis=0)
        pwt_s[part] = weighted.T.astype(BF16)
        return jnp.concatenate(picks, axis=0).astype(BF16)

    def rows_of(pick, which):
        got = jnp.dot(pick, xs[which], preferred_element_type=F32)
        return got.reshape(REL, CAP, LANES).astype(BF16)

    def first_dispatch(j):
        return pltpu.make_async_remote_copy(
            src_ref=send_s.at[0, 1, j],
            dst_ref=gx.at[0, 1, j],
            send_sem=disp_send.at[j],
            recv_sem=disp_recv.at[j],
            device_id=(my_y, place(0, j, 1)),
            device_id_type=MESH,
        )

    def dispatch(part, j):
        return pltpu.make_async_remote_copy(
            src_ref=send_s.at[part, pl.ds(0, 3), j],
            dst_ref=gx.at[part, pl.ds(0, 3), j],
            send_sem=disp_send.at[part * REL + j],
            recv_sem=disp_recv.at[part * REL + j],
            device_id=(my_y, place(part, j, 1)),
            device_id_type=MESH,
        )

    def slot(r):
        return (r + 1) % NY

    def ring(buffer, sends, recvs, half, part, step, way, first):
        to = right if way == 0 else left
        if step < 4:
            r_from = step - 1 if way == 0 else (NY + 1 - step) % NY
            r_to = step if way == 0 else NY - step
            src = buffer.at[part, first(r_from)]
            dst = buffer.at[part, first(r_to)]
        else:
            r_from = 3 if way == 0 else 5
            rows = pl.ds(0 if way == 0 else half, half)
            src = buffer.at[part, first(r_from), rows]
            dst = buffer.at[part, first(4), rows]
        sem = part * 8 + way * 4 + step - 1
        return pltpu.make_async_remote_copy(
            src_ref=src,
            dst_ref=dst,
            send_sem=sends.at[sem],
            recv_sem=recvs.at[sem],
            device_id=(to, my_e),
            device_id_type=MESH,
        )

    def x_copy(part, step, way):
        return ring(gx, x_send_s, x_recv_s, REL // 2, part, step, way, slot)

    def h_copy(part, step, way):
        return ring(gh, h_send_s, h_recv_s, HALF // 2, part, step, way, lambda r: r)

    def start(copy, part, step):
        for way in range(2):
            copy(part, step, way).start()

    def arrived(copy, part, step):
        for way in range(2):
            copy(part, step, way).wait_recv()

    def give_back(part, j):
        return pltpu.make_async_remote_copy(
            src_ref=ret_out.at[part, j],
            dst_ref=ret_in.at[part, j],
            send_sem=ret_send.at[part * REL + j],
            recv_sem=ret_recv.at[part * REL + j],
            device_id=(my_y, place(part, j, -1)),
            device_id_type=MESH,
        )

    def greet(to, which, sem):
        return pltpu.make_async_remote_copy(
            src_ref=xs.at[1],
            dst_ref=xs.at[which],
            send_sem=pre_send.at[sem],
            recv_sem=pre_recv.at[sem],
            device_id=(to, my_e),
            device_id_type=MESH,
        )

    def stat_copy(i):
        return pltpu.make_async_remote_copy(
            src_ref=stats_s.at[0],
            dst_ref=stats_s.at[i],
            send_sem=st_send.at[i],
            recv_sem=st_recv.at[i],
            device_id=((my_y + i) % NY, my_e),
            device_id_type=MESH,
        )

    pick = selection(0)
    send_s[0, 1] = rows_of(pick, 1)
    gx[0, 1, 0] = send_s[0, 1, 0]

    pl.semaphore_wait(barrier, NE - 1 + NY - 1)

    @pl.loop(1, REL)
    def _(j):
        first_dispatch(j).start()

    greet(right, 2, 0).start()
    greet(left, 0, 1).start()

    @pl.loop(1, NY)
    def _(i):
        stat_copy(i).start()

    @pl.loop(1, REL)
    def _(j):
        first_dispatch(j).wait_recv()

    start(x_copy, 0, 1)

    greet(right, 2, 0).wait_recv()
    greet(left, 0, 1).wait_recv()

    def send_part(part):
        picked = selection(part)
        for which in range(3):
            send_s[part, which] = rows_of(picked, which)

        @pl.loop(0, REL)
        def _(j):
            dispatch(part, j).start()

    send_part(1)
    arrived(x_copy, 0, 1)
    start(x_copy, 0, 2)

    for ref in (wg_s, wu_s, wd_s):
        ref[...] = jnp.zeros_like(ref)
    for k in range(NY):
        columns = slice(k * FEAT, (k + 1) * FEAT)
        wg_s[k, TAIL : TAIL + UNITS, 0:FEAT] = gate_ref[:, columns]
        wu_s[k, TAIL : TAIL + UNITS, 0:FEAT] = up_ref[:, columns]
        wd_s[k, TAIL : TAIL + UNITS, 0:FEAT] = down_ref[k * UNITS : (k + 1) * UNITS, :]
    row16 = lax.broadcasted_iota(jnp.int32, (16, 128), 0) + (SUM_ROW - SUM_ROW % 16)
    lane16 = lax.broadcasted_iota(jnp.int32, (16, 128), 1)
    ones = (row16 == SUM_ROW) & ((lane16 == at) | (lane16 == at + 1))
    ones = jnp.where(ones, 1.0, 0.0).astype(BF16)
    base = SUM_ROW - SUM_ROW % 16
    for k in range(NY):
        wg_s[k, base : base + 16, 256:LANES] = wg_s[k, base : base + 16, 256:LANES] + ones

    @pl.loop(2, PARTS)
    def _(part):
        send_part(part)

    acc_t[...] = jnp.zeros_like(acc_t)

    def x_dot(part, r):
        k = (my_y + NY - r) % NY
        block = gx[part, slot(r)].reshape(ROWS, LANES)
        for h in range(2):
            rows = slice(h * HALF, (h + 1) * HALF)
            cut = slice(TAIL, TALL) if h == 0 else slice(0, 256)
            for acc, w in ((acc_g, wg_s), (acc_u, wu_s)):
                add = lax.dot_general(block[rows], w[k, cut, :], NT, preferred_element_type=F32)
                if r == 0:
                    acc[rows] = add
                else:
                    acc[rows] += add

    def h_dot(part, r):
        k = (my_y + NY - r) % NY
        for h in range(2):
            rows = slice(h * HALF, (h + 1) * HALF)
            cut = slice(TAIL, TALL) if h == 0 else slice(0, 256)
            lanes = slice(0, 256) if h == 0 else slice(128, 384)
            add = jnp.dot(gh[part, r, :, lanes], wd_s[k, cut, :], preferred_element_type=F32)
            if r == 0:
                acc_o[rows] = add
            else:
                acc_o[rows] += add

    def activate(part):
        halves = []
        for h in range(2):
            rows = slice(h * HALF, (h + 1) * HALF)
            at_row = SUM_ROW - TAIL if h == 0 else SUM_ROW
            g, u = acc_g[rows], acc_u[rows]
            inverse = lax.rsqrt(g[:, at_row : at_row + 1] * (1.0 / D) + 1e-05)
            g = g * inverse
            u = u * inverse
            halves.append(g * jax.nn.sigmoid(1.702 * g) * (u + 1.0))
        a, b = halves
        gh[part, 0, :, 0:128] = a[:, 0:128].astype(BF16)
        gh[part, 0, :, 128:256] = (a[:, 128:256] + b[:, 0:128]).astype(BF16)
        gh[part, 0, :, 256:384] = b[:, 128:256].astype(BF16)

    def send_back(part):
        ret_out[part] = acc_o[...].reshape(REL, CAP, LANES).astype(BF16)

        @pl.when(part == 0)
        def _():
            ret_in[0, 0] = ret_out[0, 0]

        @pl.loop(jnp.where(part == 0, 1, 0), REL)
        def _(j):
            give_back(part, j).start()

    def combine(part):
        @pl.loop(jnp.where(part == 0, 1, 0), REL)
        def _(j):
            give_back(part, j).wait_recv()

        acc_t[...] += jnp.dot(
            pwt_s[part], ret_in[part].reshape(ROWS, LANES), preferred_element_type=F32
        )

    @pl.loop(0, PARTS + 2)
    def _(i):
        has_x = i < PARTS
        has_h = (i >= 1) & (i < PARTS + 1)

        @pl.when(has_x)
        def _():
            arrived(x_copy, i, 2)
            start(x_copy, i, 3)

        @pl.when(i + 1 < PARTS)
        def _():
            @pl.loop(0, REL)
            def _(j):
                dispatch(i + 1, j).wait_recv()

            start(x_copy, i + 1, 2)

        @pl.when(has_h)
        def _():
            arrived(h_copy, i - 1, 1)
            start(h_copy, i - 1, 2)

        @pl.when(has_x)
        def _():
            for r in (0, 1, 7):
                x_dot(i, r)

        @pl.when(i >= 2)
        def _():
            arrived(h_copy, i - 2, 4)
            h_dot(i - 2, 4)
            send_back(i - 2)

        @pl.when(has_x)
        def _():
            for r in (2, 6):
                x_dot(i, r)
            arrived(x_copy, i, 3)
            start(x_copy, i, 4)

        @pl.when(has_h)
        def _():
            arrived(h_copy, i - 1, 2)
            start(h_copy, i - 1, 3)

        @pl.when(has_x)
        def _():
            for r in (3, 5):
                x_dot(i, r)

        @pl.when(has_h)
        def _():
            for r in (0, 1, 7):
                h_dot(i - 1, r)

        @pl.when(has_x)
        def _():
            arrived(x_copy, i, 4)
            x_dot(i, 4)
            activate(i)
            start(h_copy, i, 1)

        @pl.when(has_h)
        def _():
            arrived(h_copy, i - 1, 3)
            start(h_copy, i - 1, 4)
            for r in (2, 6, 3, 5):
                h_dot(i - 1, r)

        @pl.when(i >= 3)
        def _():
            combine(i - 3)

    @pl.loop(1, NY)
    def _(i):
        stat_copy(i).wait_recv()

    sums = stats_s[0]
    most = stats_s[0]
    for i in range(1, NY):
        sums = sums + stats_s[i]
        most = jnp.maximum(most, stats_s[i])
    peaks_ref[...] = most[1:2, :] * lax.rsqrt(sums[0:1, :] * (1.0 / D) + 1e-05)

    combine(PARTS - 1)
    out_ref[...] = acc_t[:, 0:FEAT].astype(BF16)

    @pl.loop(1, REL)
    def _(j):
        first_dispatch(j).wait_send()

    @pl.loop(1, PARTS)
    def _(part):
        @pl.loop(0, REL)
        def _(j):
            dispatch(part, j).wait_send()

        for way in range(2):
            for step in (2, 3, 4):
                x_copy(part, step, way).wait_send()

    for way in range(2):
        for step in (1, 2, 3, 4):
            x_copy(0, step, way).wait_send()

    @pl.loop(0, PARTS)
    def _(part):
        for way in range(2):
            for step in (1, 2, 3, 4):
                h_copy(part, step, way).wait_send()

        @pl.loop(jnp.where(part == 0, 1, 0), REL)
        def _(j):
            give_back(part, j).wait_send()

    greet(right, 2, 0).wait_send()
    greet(left, 0, 1).wait_send()

    @pl.loop(1, NY)
    def _(i):
        stat_copy(i).wait_send()


def shards(hidden_in, norm_gain, expert_ids, route_weights, gate_weight, up_weight, down_weight):
    vmem = pl.BlockSpec(memory_space=pltpu.VMEM)
    dma = pltpu.SemaphoreType.DMA
    out, peaks = pl.pallas_call(
        kernel,
        out_shape=(
            jax.ShapeDtypeStruct((TOK, FEAT), BF16),
            jax.ShapeDtypeStruct((1, TOK), F32),
        ),
        in_specs=[vmem] * 7,
        out_specs=(vmem, vmem),
        scratch_shapes=[
            pltpu.VMEM((3, TOK, LANES), BF16),
            pltpu.VMEM((NE, TOK), F32),
            pltpu.VMEM((NE, TOK), F32),
            pltpu.VMEM((PARTS, TOK, ROWS), BF16),
            pltpu.VMEM((PARTS, 3, REL, CAP, LANES), BF16),
            pltpu.VMEM((PARTS, NY, REL, CAP, LANES), BF16),
            pltpu.VMEM((PARTS, NY, HALF, LANES), BF16),
            pltpu.VMEM((NY, TALL, LANES), BF16),
            pltpu.VMEM((NY, TALL, LANES), BF16),
            pltpu.VMEM((NY, TALL, LANES), BF16),
            pltpu.VMEM((PARTS, REL, CAP, LANES), BF16),
            pltpu.VMEM((PARTS, REL, CAP, LANES), BF16),
            pltpu.VMEM((NY, 8, TOK), F32),
            pltpu.VMEM((ROWS, 256), F32),
            pltpu.VMEM((ROWS, 256), F32),
            pltpu.VMEM((ROWS, LANES), F32),
            pltpu.VMEM((TOK, LANES), F32),
            dma((2,)),
            dma((2,)),
            dma((NE,)),
            dma((NE,)),
            dma((PARTS * 8,)),
            dma((PARTS * 8,)),
            dma((PARTS * 8,)),
            dma((PARTS * 8,)),
            dma((NE,)),
            dma((NE,)),
            dma((NY,)),
            dma((NY,)),
        ],
        compiler_params=pltpu.CompilerParams(
            collective_id=0, has_side_effects=True, vmem_limit_bytes=58 * 2**20
        ),
    )(
        hidden_in,
        norm_gain.reshape(1, FEAT),
        expert_ids,
        route_weights,
        gate_weight[0],
        up_weight[0],
        down_weight[0],
    )
    return (out, peaks.reshape(TOK))


def solution(mesh):
    in_specs = (
        P("expert", "dp"),
        P("dp"),
        P("expert", None),
        P("expert", None),
        P("expert", "dp", None),
        P("expert", "dp", None),
        P("expert", None, "dp"),
    )
    out_specs = (P("expert", "dp"), P("expert"))
    return jax.shard_map(shards, mesh=mesh, in_specs=in_specs, out_specs=out_specs, check_vma=False)
```

```python
import jax
import jax.numpy as jnp
from jax import lax
from jax.experimental import pallas as pl
from jax.experimental.pallas import tpu as pltpu
from jax.sharding import PartitionSpec as P

D = 2880
TOP = 4
CAP = 24
MESH = pl.DeviceIdType.MESH
F32 = jnp.float32
BF16 = jnp.bfloat16

NY = 8
NX, NZ, NC = 4, 8, 2
NE = NX * NZ * NC
PARTS = NX * NC
REL = NZ
ROWS = REL * CAP
HALF = ROWS // 2
TOK = 256
FEAT = D // NY
UNITS = 180
LANES = 384
TAIL = 64
TALL = 320
SUM_ROW = 184
WIDE = 256
PLAIN = 1
AHEAD = PLAIN + 2
NT = (((1,), (1,)), ((), ()))


def kernel(
    hid_ref, gain_ref, ids_ref, rw_ref, gate_ref, up_ref, down_ref,
    out_ref, peaks_ref,
    xs, key_s, wsel_s, pwt_s, send_s, gx, gh, wx_s, wd_s, ret_out, ret_in, stats_s,
    acc_x, acc_o, acc_t,
    pre_send, pre_recv, disp_send, disp_recv, x_send_s, x_recv_s, h_send_s, h_recv_s,
    ret_send, ret_recv, st_send, st_recv,
):
    my_y = lax.axis_index("dp")
    my_e = lax.axis_index("expert")
    my_x = my_e // (NZ * NC)
    my_z = (my_e // NC) % NZ
    my_c = my_e % NC
    right = (my_y + 1) % NY
    left = (my_y + NY - 1) % NY

    barrier = pltpu.get_barrier_semaphore()

    @pl.loop(1, NE)
    def _(i):
        pl.semaphore_signal(
            barrier, inc=1, device_id=(my_y, (my_e + i) % NE), device_id_type=MESH
        )

    @pl.loop(1, NY)
    def _(i):
        pl.semaphore_signal(
            barrier, inc=1, device_id=((my_y + i) % NY, my_e), device_id_type=MESH
        )

    gain = jnp.broadcast_to(gain_ref[...].reshape(1, FEAT), (128, FEAT))
    gain = jnp.concatenate([gain, jnp.zeros((128, LANES - FEAT), F32)], axis=1).T[0:FEAT, :]
    hid = hid_ref[...].astype(F32)
    scaled = hid * jnp.concatenate([gain, gain], axis=1)
    total = jnp.sum(hid * hid, axis=0, keepdims=True)
    biggest = jnp.max(jnp.abs(scaled), axis=0, keepdims=True)
    high = total.astype(BF16).astype(F32)
    row = lax.broadcasted_iota(jnp.int32, (LANES - FEAT, TOK), 0)
    extra = jnp.where(row == 0, high, jnp.where(row == 1, total - high, 0.0))
    xs[1] = jnp.concatenate([scaled, extra], axis=0).astype(BF16)
    row8 = lax.broadcasted_iota(jnp.int32, (8, TOK), 0)
    stats_s[0] = jnp.where(row8 == 0, total, jnp.where(row8 == 1, biggest, 0.0))

    expert = lax.broadcasted_iota(jnp.int32, (NE, TOK), 0)
    named = jnp.zeros((NE, TOK), F32)
    weight = jnp.zeros((NE, TOK), F32)
    for j in range(TOP):
        hit = ids_ref[j : j + 1, :] == expert
        named = jnp.where(hit, 1.0, named)
        weight = jnp.where(hit, rw_ref[j : j + 1, :], weight)
    wsel_s[...] = weight
    earlier = (
        lax.broadcasted_iota(jnp.int32, (TOK, TOK), 0)
        < lax.broadcasted_iota(jnp.int32, (TOK, TOK), 1)
    )
    earlier = jnp.where(earlier, 1.0, 0.0).astype(BF16)
    before = jnp.dot(named.astype(BF16), earlier, preferred_element_type=F32)
    key_s[...] = jnp.where(named > 0.5, before, -1.0)

    def place(part, j, sign):
        dx, dc = part // NC, part % NC
        x = (my_x + NX + sign * dx) % NX
        z = (my_z + NZ + sign * j) % NZ
        c = (my_c + dc) % NC
        return (x * NZ + z) * NC + c

    rank = lax.broadcasted_iota(jnp.int32, (CAP, TOK), 0).astype(F32)

    def selection(part):
        picks, weighted = [], []
        for j in range(REL):
            e = place(part, j, 1)
            hit = key_s[pl.ds(e, 1), :] == rank
            picks.append(jnp.where(hit, 1.0, 0.0))
            weighted.append(jnp.where(hit, wsel_s[pl.ds(e, 1), :], 0.0))
        weighted = jnp.concatenate(weighted, axis=0)
        pwt_s[part] = weighted.T.astype(BF16)
        return jnp.concatenate(picks, axis=0).astype(BF16)

    def rows_of(pick, which):
        got = lax.dot_general(pick, xs[which], NT, preferred_element_type=F32)
        return got.reshape(REL, CAP, LANES).astype(BF16)

    def first(part):
        return jnp.where(part == 0, 1, 0)

    def plain_dispatch(part, j):
        return pltpu.make_async_remote_copy(
            src_ref=send_s.at[part, 1, j],
            dst_ref=gx.at[part, 1, j],
            send_sem=disp_send.at[part * REL + j],
            recv_sem=disp_recv.at[part * REL + j],
            device_id=(my_y, place(part, j, 1)),
            device_id_type=MESH,
        )

    def dispatch(part, j):
        return pltpu.make_async_remote_copy(
            src_ref=send_s.at[part, pl.ds(0, 3), j],
            dst_ref=gx.at[part, pl.ds(0, 3), j],
            send_sem=disp_send.at[part * REL + j],
            recv_sem=disp_recv.at[part * REL + j],
            device_id=(my_y, place(part, j, 1)),
            device_id_type=MESH,
        )

    def slot(r):
        return (r + 1) % NY

    def ring(buffer, sends, recvs, half, part, step, way, where):
        to = right if way == 0 else left
        if step < 4:
            r_from = step - 1 if way == 0 else (NY + 1 - step) % NY
            r_to = step if way == 0 else NY - step
            src = buffer.at[part, where(r_from)]
            dst = buffer.at[part, where(r_to)]
        else:
            r_from = 3 if way == 0 else 5
            rows = pl.ds(0 if way == 0 else half, half)
            src = buffer.at[part, where(r_from), rows]
            dst = buffer.at[part, where(4), rows]
        sem = part * 8 + way * 4 + step - 1
        return pltpu.make_async_remote_copy(
            src_ref=src,
            dst_ref=dst,
            send_sem=sends.at[sem],
            recv_sem=recvs.at[sem],
            device_id=(to, my_e),
            device_id_type=MESH,
        )

    def x_copy(part, step, way):
        return ring(gx, x_send_s, x_recv_s, REL // 2, part, step, way, slot)

    def h_copy(part, step, way):
        return ring(gh, h_send_s, h_recv_s, HALF // 2, part, step, way, lambda r: r)

    def start(copy, part, step):
        for way in range(2):
            copy(part, step, way).start()

    def arrived(copy, part, step):
        for way in range(2):
            copy(part, step, way).wait_recv()

    def left_here(copy, part, steps):
        for way in range(2):
            for step in steps:
                copy(part, step, way).wait_send()

    def give_back(part, j):
        return pltpu.make_async_remote_copy(
            src_ref=ret_out.at[part, j],
            dst_ref=ret_in.at[part, j],
            send_sem=ret_send.at[part * REL + j],
            recv_sem=ret_recv.at[part * REL + j],
            device_id=(my_y, place(part, j, -1)),
            device_id_type=MESH,
        )

    def greet(to, which, sem):
        return pltpu.make_async_remote_copy(
            src_ref=xs.at[1],
            dst_ref=xs.at[which],
            send_sem=pre_send.at[sem],
            recv_sem=pre_recv.at[sem],
            device_id=(to, my_e),
            device_id_type=MESH,
        )

    def stat_copy(i):
        return pltpu.make_async_remote_copy(
            src_ref=stats_s.at[0],
            dst_ref=stats_s.at[i],
            send_sem=st_send.at[i],
            recv_sem=st_recv.at[i],
            device_id=((my_y + i) % NY, my_e),
            device_id_type=MESH,
        )

    send_s[0, 1] = rows_of(selection(0), 1)
    gx[0, 1, 0] = send_s[0, 1, 0]
    for part in range(1, PLAIN):
        send_s[part, 1] = rows_of(selection(part), 1)

    pl.semaphore_wait(barrier, NE - 1 + NY - 1)

    greet(right, 2, 0).start()
    greet(left, 0, 1).start()
    for part in range(PLAIN):
        @pl.loop(first(part), REL)
        def _(j):
            plain_dispatch(part, j).start()

    @pl.loop(1, NY)
    def _(i):
        stat_copy(i).start()

    wx_s[...] = jnp.zeros_like(wx_s)
    for k in range(NY):
        columns = slice(k * FEAT, (k + 1) * FEAT)
        wx_s[k, 0:UNITS, 0:FEAT] = gate_ref[:, columns]
        wx_s[k, WIDE : WIDE + UNITS, 0:FEAT] = up_ref[:, columns]

    for part in range(PLAIN):
        @pl.loop(first(part), REL)
        def _(j):
            plain_dispatch(part, j).wait_recv()

        start(x_copy, part, 1)

    greet(right, 2, 0).wait_recv()
    greet(left, 0, 1).wait_recv()

    def send_part(part):
        picked = selection(part)
        for which in range(3):
            send_s[part, which] = rows_of(picked, which)

        @pl.loop(0, REL)
        def _(j):
            dispatch(part, j).start()

    @pl.loop(PLAIN, AHEAD)
    def _(part):
        send_part(part)

    def prepare():
        base = SUM_ROW - SUM_ROW % 16
        row16 = lax.broadcasted_iota(jnp.int32, (16, 128), 0) + base
        lane16 = lax.broadcasted_iota(jnp.int32, (16, 128), 1) + 256
        ones = (row16 == SUM_ROW) & ((lane16 == FEAT) | (lane16 == FEAT + 1))
        ones = jnp.where(ones, 1.0, 0.0).astype(BF16)
        for k in range(NY):
            wx_s[k, base : base + 16, 256:LANES] = wx_s[k, base : base + 16, 256:LANES] + ones
        wd_s[...] = jnp.zeros_like(wd_s)
        for k in range(NY):
            wd_s[k, TAIL : TAIL + UNITS, 0:FEAT] = down_ref[k * UNITS : (k + 1) * UNITS, :]
        acc_t[...] = jnp.zeros_like(acc_t)

    def x_dot(part, r):
        k = (my_y + NY - r) % NY
        block = gx[part, slot(r)].reshape(ROWS, LANES)
        add = lax.dot_general(block, wx_s[k], NT, preferred_element_type=F32)
        if r == 0:
            acc_x[...] = add
        else:
            acc_x[...] += add

    def h_dot(part, r):
        k = (my_y + NY - r) % NY
        for h in range(2):
            rows = slice(h * HALF, (h + 1) * HALF)
            cut = slice(TAIL, TALL) if h == 0 else slice(0, 256)
            lanes = slice(0, 256) if h == 0 else slice(128, 384)
            add = jnp.dot(gh[part, r, :, lanes], wd_s[k, cut, :], preferred_element_type=F32)
            if r == 0:
                acc_o[rows] = add
            else:
                acc_o[rows] += add

    def activate(part):
        g, u = acc_x[:, 0:WIDE], acc_x[:, WIDE : 2 * WIDE]
        inverse = lax.rsqrt(g[:, SUM_ROW : SUM_ROW + 1] * (1.0 / D) + 1e-05)
        g = g * inverse
        u = u * inverse
        hidden = g * jax.nn.sigmoid(1.702 * g) * (u + 1.0)
        a = hidden[0:HALF]
        b = pltpu.roll(hidden[HALF:ROWS], TAIL, 1)
        gh[part, 0, :, 0:128] = a[:, 0:128].astype(BF16)
        lane = lax.broadcasted_iota(jnp.int32, (HALF, 128), 1)
        middle = jnp.where(lane < TAIL, a[:, 128:256], b[:, 0:128])
        gh[part, 0, :, 128:256] = middle.astype(BF16)
        gh[part, 0, :, 256:384] = b[:, 128:256].astype(BF16)

    def send_back(part):
        ret_out[part] = acc_o[...].reshape(REL, CAP, LANES).astype(BF16)

        @pl.when(part == 0)
        def _():
            ret_in[0, 0] = ret_out[0, 0]

        @pl.loop(first(part), REL)
        def _(j):
            give_back(part, j).start()

    def combine(part):
        @pl.loop(first(part), REL)
        def _(j):
            give_back(part, j).wait_recv()

        acc_t[...] += jnp.dot(
            pwt_s[part], ret_in[part].reshape(ROWS, LANES), preferred_element_type=F32
        )

    @pl.loop(0, PARTS + 3)
    def _(i):
        in_x = i < PARTS
        in_x4 = (i >= 1) & (i <= PARTS)
        in_h = (i >= 2) & (i <= PARTS + 1)
        in_h4 = i >= 3

        @pl.when(i < PLAIN)
        def _():
            arrived(x_copy, i, 1)

        @pl.when((i >= PLAIN) & in_x)
        def _():
            @pl.loop(0, REL)
            def _(j):
                dispatch(i, j).wait_recv()

        @pl.when(in_x)
        def _():
            start(x_copy, i, 2)

        @pl.when(in_x4)
        def _():
            arrived(x_copy, i - 1, 3)
            start(x_copy, i - 1, 4)

        @pl.when(in_h)
        def _():
            arrived(h_copy, i - 2, 1)
            start(h_copy, i - 2, 2)

        @pl.when(in_h4)
        def _():
            arrived(h_copy, i - 3, 3)
            start(h_copy, i - 3, 4)

        @pl.when(i == 0)
        def _():
            prepare()

        @pl.when(i + AHEAD < PARTS)
        def _():
            send_part(i + AHEAD)

        @pl.when(in_x4)
        def _():
            for r in (0, 1, 7, 2, 6, 3, 5):
                x_dot(i - 1, r)

        @pl.when(in_x)
        def _():
            arrived(x_copy, i, 2)
            start(x_copy, i, 3)

        @pl.when(in_x4)
        def _():
            arrived(x_copy, i - 1, 4)
            x_dot(i - 1, 4)
            activate(i - 1)
            start(h_copy, i - 1, 1)

        @pl.when(in_h)
        def _():
            arrived(h_copy, i - 2, 2)
            start(h_copy, i - 2, 3)

        @pl.when(in_h4)
        def _():
            for r in (0, 1, 7, 2, 6, 3, 5):
                h_dot(i - 3, r)
            arrived(h_copy, i - 3, 4)
            h_dot(i - 3, 4)
            send_back(i - 3)

        @pl.when(i >= 4)
        def _():
            combine(i - 4)
            left_here(h_copy, i - 4, (1, 2, 3, 4))

            @pl.loop(first(i - 4), REL)
            def _(j):
                give_back(i - 4, j).wait_send()

        @pl.when((i >= 2) & (i < PARTS + 2))
        def _():
            left_here(x_copy, i - 2, (2, 3, 4))

        @pl.when(i < PLAIN)
        def _():
            left_here(x_copy, i, (1,))

            @pl.loop(first(i), REL)
            def _(j):
                plain_dispatch(i, j).wait_send()

        @pl.when((i >= PLAIN) & in_x)
        def _():
            @pl.loop(0, REL)
            def _(j):
                dispatch(i, j).wait_send()

        @pl.when(i == 3)
        def _():
            greet(right, 2, 0).wait_send()
            greet(left, 0, 1).wait_send()

            @pl.loop(1, NY)
            def _(n):
                stat_copy(n).wait()

            sums = stats_s[0]
            most = stats_s[0]
            for n in range(1, NY):
                sums = sums + stats_s[n]
                most = jnp.maximum(most, stats_s[n])
            peaks = most[1:2, :] * lax.rsqrt(sums[0:1, :] * (1.0 / D) + 1e-05)
            peaks_ref[...] = peaks.reshape(peaks_ref.shape)

    left_here(h_copy, PARTS - 1, (1, 2, 3, 4))
    combine(PARTS - 1)
    out_ref[...] = acc_t[...].T[0:FEAT, :].astype(BF16)

    @pl.loop(0, REL)
    def _(j):
        give_back(PARTS - 1, j).wait_send()


def shards(hidden_in, norm_gain, expert_ids, route_weights, gate_weight, up_weight, down_weight):
    vmem = pl.BlockSpec(memory_space=pltpu.VMEM)
    dma = pltpu.SemaphoreType.DMA
    out, peaks = pl.pallas_call(
        kernel,
        out_shape=(
            jax.ShapeDtypeStruct((FEAT, TOK), BF16),
            jax.ShapeDtypeStruct((TOK,), F32),
        ),
        in_specs=[vmem] * 7,
        out_specs=(vmem, vmem),
        scratch_shapes=[
            pltpu.VMEM((3, LANES, TOK), BF16),
            pltpu.VMEM((NE, TOK), F32),
            pltpu.VMEM((NE, TOK), F32),
            pltpu.VMEM((PARTS, TOK, ROWS), BF16),
            pltpu.VMEM((PARTS, 3, REL, CAP, LANES), BF16),
            pltpu.VMEM((PARTS, NY, REL, CAP, LANES), BF16),
            pltpu.VMEM((PARTS, NY, HALF, LANES), BF16),
            pltpu.VMEM((NY, 2 * WIDE, LANES), BF16),
            pltpu.VMEM((NY, TALL, LANES), BF16),
            pltpu.VMEM((PARTS, REL, CAP, LANES), BF16),
            pltpu.VMEM((PARTS, REL, CAP, LANES), BF16),
            pltpu.VMEM((NY, 8, TOK), F32),
            pltpu.VMEM((ROWS, 2 * WIDE), F32),
            pltpu.VMEM((ROWS, LANES), F32),
            pltpu.VMEM((TOK, LANES), F32),
            dma((2,)),
            dma((2,)),
            dma((NE,)),
            dma((NE,)),
            dma((PARTS * 8,)),
            dma((PARTS * 8,)),
            dma((PARTS * 8,)),
            dma((PARTS * 8,)),
            dma((NE,)),
            dma((NE,)),
            dma((NY,)),
            dma((NY,)),
        ],
        compiler_params=pltpu.CompilerParams(
            collective_id=0, has_side_effects=True, vmem_limit_bytes=58 * 2**20
        ),
    )(
        hidden_in.T,
        norm_gain,
        expert_ids.T,
        route_weights.T,
        gate_weight[0],
        up_weight[0],
        down_weight[0],
    )
    return (out.T, peaks)


def solution(mesh):
    in_specs = (
        P("expert", "dp"),
        P("dp"),
        P("expert", None),
        P("expert", None),
        P("expert", "dp", None),
        P("expert", "dp", None),
        P("expert", None, "dp"),
    )
    out_specs = (P("expert", "dp"), P("expert"))
    return jax.shard_map(shards, mesh=mesh, in_specs=in_specs, out_specs=out_specs, check_vma=False)
```

```python
import jax
import jax.numpy as jnp
from jax import lax
from jax.experimental import pallas as pl
from jax.experimental.pallas import tpu as pltpu
from jax.sharding import PartitionSpec as P

D = 2880
TOP = 4
CAP = 24
MESH = pl.DeviceIdType.MESH
F32 = jnp.float32
BF16 = jnp.bfloat16

NY = 8
NX, NZ, NC = 4, 8, 2
NE = NX * NZ * NC
PARTS = NX * NC
LAST = PARTS - 1
BROAD = 6
REL = NZ
ROWS = REL * CAP
HALF = ROWS // 2
TOK = 256
FEAT = D // NY
UNITS = 180
LANES = 384
TAIL = 64
TALL = 320
SUM_ROW = 184
WIDE = 256
AHEAD = 4
OWN = 2
NT = (((1,), (1,)), ((), ()))


def kernel(
    hid_ref, gain_ref, ids_ref, rw_ref, gate_ref, up_ref, down_ref,
    out_ref, peaks_ref,
    xs, key_s, wsel_s, pwt_s, send_s, gx, gh, wx_s, wd_s, ret_out, ret_in, stats_s,
    acc_x, acc_o, acc_t,
    pre_send, pre_recv, disp_send, disp_recv, side_send, side_recv, x_send_s, x_recv_s, h_send_s, h_recv_s,
    ret_send, ret_recv, st_send, st_recv,
):
    my_y = lax.axis_index("dp")
    my_e = lax.axis_index("expert")
    my_x = my_e // (NZ * NC)
    my_z = (my_e // NC) % NZ
    my_c = my_e % NC
    right = (my_y + 1) % NY
    left = (my_y + NY - 1) % NY

    barrier = pltpu.get_barrier_semaphore()

    @pl.loop(1, NE)
    def _(i):
        pl.semaphore_signal(
            barrier, inc=1, device_id=(my_y, (my_e + i) % NE), device_id_type=MESH
        )

    @pl.loop(1, NY)
    def _(i):
        pl.semaphore_signal(
            barrier, inc=1, device_id=((my_y + i) % NY, my_e), device_id_type=MESH
        )

    gain = jnp.broadcast_to(gain_ref[...].reshape(1, FEAT), (128, FEAT))
    gain = jnp.concatenate([gain, jnp.zeros((128, LANES - FEAT), F32)], axis=1).T[0:FEAT, :]
    hid = hid_ref[...].astype(F32)
    scaled = hid * jnp.concatenate([gain, gain], axis=1)
    total = jnp.sum(hid * hid, axis=0, keepdims=True)
    biggest = jnp.max(jnp.abs(scaled), axis=0, keepdims=True)
    high = total.astype(BF16).astype(F32)
    row = lax.broadcasted_iota(jnp.int32, (LANES - FEAT, TOK), 0)
    extra = jnp.where(row == 0, high, jnp.where(row == 1, total - high, 0.0))
    xs[OWN] = jnp.concatenate([scaled, extra], axis=0).astype(BF16)
    row8 = lax.broadcasted_iota(jnp.int32, (8, TOK), 0)
    stats_s[0] = jnp.where(row8 == 0, total, jnp.where(row8 == 1, biggest, 0.0))

    expert = lax.broadcasted_iota(jnp.int32, (NE, TOK), 0)
    named = jnp.zeros((NE, TOK), F32)
    weight = jnp.zeros((NE, TOK), F32)
    for j in range(TOP):
        hit = ids_ref[j : j + 1, :] == expert
        named = jnp.where(hit, 1.0, named)
        weight = jnp.where(hit, rw_ref[j : j + 1, :], weight)
    wsel_s[...] = weight
    earlier = (
        lax.broadcasted_iota(jnp.int32, (TOK, TOK), 0)
        < lax.broadcasted_iota(jnp.int32, (TOK, TOK), 1)
    )
    earlier = jnp.where(earlier, 1.0, 0.0).astype(BF16)
    before = jnp.dot(named.astype(BF16), earlier, preferred_element_type=F32)
    key_s[...] = jnp.where(named > 0.5, before, -1.0)

    def place(part, j, sign):
        turn = (part + 1) % PARTS
        dx, dc, dz = turn // NC, turn % NC, j
        x = (my_x + NX + sign * dx) % NX
        z = (my_z + NZ + sign * dz) % NZ
        c = (my_c + dc) % NC
        return (x * NZ + z) * NC + c

    rank = lax.broadcasted_iota(jnp.int32, (CAP, TOK), 0).astype(F32)

    def selection(part):
        picks, weighted = [], []
        for j in range(REL):
            e = place(part, j, 1)
            hit = key_s[pl.ds(e, 1), :] == rank
            picks.append(jnp.where(hit, 1.0, 0.0))
            weighted.append(jnp.where(hit, wsel_s[pl.ds(e, 1), :], 0.0))
        weighted = jnp.concatenate(weighted, axis=0)
        pwt_s[part] = weighted.T.astype(BF16)
        return jnp.concatenate(picks, axis=0).astype(BF16)

    def rows_of(pick, which):
        got = lax.dot_general(pick, xs[which], NT, preferred_element_type=F32)
        return got.reshape(REL, CAP, LANES).astype(BF16)

    def first(part):
        return jnp.where(part == LAST, 1, 0)

    def row_copy(part, j, slots, send, recv, sem):
        return pltpu.make_async_remote_copy(
            src_ref=send_s.at[part, slots, j],
            dst_ref=gx.at[part, slots, j],
            send_sem=send.at[sem],
            recv_sem=recv.at[sem],
            device_id=(my_y, place(part, j, 1)),
            device_id_type=MESH,
        )

    def own_rows(part, j):
        return row_copy(part, j, OWN, disp_send, disp_recv, part * REL + j)

    def near_rows(part, j):
        return row_copy(part, j, pl.ds(OWN - 1, 3), disp_send, disp_recv, part * REL + j)

    def wide_rows(part, j):
        return row_copy(part, j, pl.ds(0, 5), disp_send, disp_recv, part * REL + j)

    def side_rows(j, way):
        return row_copy(1, j, OWN - 1 + 2 * way, side_send, side_recv, way * REL + j)

    def slot(r):
        return (r + OWN) % NY

    def ring(buffer, sends, recvs, half, part, step, way, where):
        to = right if way == 0 else left
        if step < 4:
            r_from = step - 1 if way == 0 else (NY + 1 - step) % NY
            r_to = step if way == 0 else NY - step
            src = buffer.at[part, where(r_from)]
            dst = buffer.at[part, where(r_to)]
        else:
            r_from = 3 if way == 0 else 5
            rows = pl.ds(0 if way == 0 else half, half)
            src = buffer.at[part, where(r_from), rows]
            dst = buffer.at[part, where(4), rows]
        sem = part * 8 + way * 4 + step - 1
        return pltpu.make_async_remote_copy(
            src_ref=src,
            dst_ref=dst,
            send_sem=sends.at[sem],
            recv_sem=recvs.at[sem],
            device_id=(to, my_e),
            device_id_type=MESH,
        )

    def x_copy(part, step, way):
        return ring(gx, x_send_s, x_recv_s, REL // 2, part, step, way, slot)

    def h_copy(part, step, way):
        return ring(gh, h_send_s, h_recv_s, HALF // 2, part, step, way, lambda r: r)

    def start(copy, part, step):
        for way in range(2):
            copy(part, step, way).start()

    def arrived(copy, part, step):
        for way in range(2):
            copy(part, step, way).wait_recv()

    def left_here(copy, part, steps):
        for way in range(2):
            for step in steps:
                copy(part, step, way).wait_send()

    def give_back(part, j):
        return pltpu.make_async_remote_copy(
            src_ref=ret_out.at[part, j],
            dst_ref=ret_in.at[part, j],
            send_sem=ret_send.at[part * REL + j],
            recv_sem=ret_recv.at[part * REL + j],
            device_id=(my_y, place(part, j, -1)),
            device_id_type=MESH,
        )

    def greet(step, way):
        to, turn = (right, 1) if way == 0 else (left, -1)
        return pltpu.make_async_remote_copy(
            src_ref=xs.at[OWN + turn * (step - 1)],
            dst_ref=xs.at[OWN + turn * step],
            send_sem=pre_send.at[way * 2 + step - 1],
            recv_sem=pre_recv.at[way * 2 + step - 1],
            device_id=(to, my_e),
            device_id_type=MESH,
        )

    def stat_copy(i):
        return pltpu.make_async_remote_copy(
            src_ref=stats_s.at[0],
            dst_ref=stats_s.at[i],
            send_sem=st_send.at[i],
            recv_sem=st_recv.at[i],
            device_id=((my_y + i) % NY, my_e),
            device_id_type=MESH,
        )

    send_s[0, OWN] = rows_of(selection(0), OWN)
    second = selection(1)
    send_s[1, OWN] = rows_of(second, OWN)

    pl.semaphore_wait(barrier, NE - 1 + NY - 1)

    greet(1, 0).start()
    greet(1, 1).start()

    @pl.loop(0, 2)
    def _(part):
        @pl.loop(0, REL)
        def _(j):
            own_rows(part, j).start()

    @pl.loop(1, NY)
    def _(i):
        stat_copy(i).start()

    wx_s[...] = jnp.zeros_like(wx_s)
    for k in range(NY):
        columns = slice(k * FEAT, (k + 1) * FEAT)
        wx_s[k, 0:UNITS, 0:FEAT] = gate_ref[:, columns]
        wx_s[k, WIDE : WIDE + UNITS, 0:FEAT] = up_ref[:, columns]

    @pl.loop(0, REL)
    def _(j):
        own_rows(0, j).wait_recv()

    start(x_copy, 0, 1)

    for way in range(2):
        greet(1, way).wait_recv()
        greet(2, way).start()

    for way in range(2):
        send_s[1, OWN - 1 + 2 * way] = rows_of(second, OWN - 1 + 2 * way)

        @pl.loop(0, REL)
        def _(j):
            side_rows(j, way).start()

    def send_part(part):
        picked = selection(part)
        for which in (OWN - 1, OWN, OWN + 1):
            send_s[part, which] = rows_of(picked, which)

        @pl.loop(0, REL)
        def _(j):
            near_rows(part, j).start()

    def send_wide(part):
        @pl.when(part == BROAD)
        def _():
            for way in range(2):
                greet(2, way).wait_recv()

        picked = selection(part)
        for which in range(5):
            send_s[part, which] = rows_of(picked, which)

        @pl.when(part == LAST)
        def _():
            for which in range(5):
                gx[LAST, which, 0] = send_s[LAST, which, 0]

        @pl.loop(first(part), REL)
        def _(j):
            wide_rows(part, j).start()

    @pl.loop(2, AHEAD)
    def _(part):
        send_part(part)

    def prepare():
        base = SUM_ROW - SUM_ROW % 16
        row16 = lax.broadcasted_iota(jnp.int32, (16, 128), 0) + base
        lane16 = lax.broadcasted_iota(jnp.int32, (16, 128), 1) + 256
        ones = (row16 == SUM_ROW) & ((lane16 == FEAT) | (lane16 == FEAT + 1))
        ones = jnp.where(ones, 1.0, 0.0).astype(BF16)
        for k in range(NY):
            wx_s[k, base : base + 16, 256:LANES] = wx_s[k, base : base + 16, 256:LANES] + ones
        wd_s[...] = jnp.zeros_like(wd_s)
        for k in range(NY):
            wd_s[k, TAIL : TAIL + UNITS, 0:FEAT] = down_ref[k * UNITS : (k + 1) * UNITS, :]
        acc_t[...] = jnp.zeros_like(acc_t)

    def x_dot(part, r):
        k = (my_y + NY - r) % NY
        block = gx[part, slot(r)].reshape(ROWS, LANES)
        add = lax.dot_general(block, wx_s[k], NT, preferred_element_type=F32)
        if r == 0:
            acc_x[...] = add
        else:
            acc_x[...] += add

    def h_dot(part, r):
        k = (my_y + NY - r) % NY
        for h in range(2):
            rows = slice(h * HALF, (h + 1) * HALF)
            cut = slice(TAIL, TALL) if h == 0 else slice(0, 256)
            lanes = slice(0, 256) if h == 0 else slice(128, 384)
            add = jnp.dot(gh[part, r, :, lanes], wd_s[k, cut, :], preferred_element_type=F32)
            if r == 0:
                acc_o[rows] = add
            else:
                acc_o[rows] += add

    def activate(part):
        g, u = acc_x[:, 0:WIDE], acc_x[:, WIDE : 2 * WIDE]
        inverse = lax.rsqrt(g[:, SUM_ROW : SUM_ROW + 1] * (1.0 / D) + 1e-05)
        g = g * inverse
        u = u * inverse
        hidden = g * jax.nn.sigmoid(1.702 * g) * (u + 1.0)
        a = hidden[0:HALF]
        b = pltpu.roll(hidden[HALF:ROWS], TAIL, 1)
        gh[part, 0, :, 0:128] = a[:, 0:128].astype(BF16)
        lane = lax.broadcasted_iota(jnp.int32, (HALF, 128), 1)
        middle = jnp.where(lane < TAIL, a[:, 128:256], b[:, 0:128])
        gh[part, 0, :, 128:256] = middle.astype(BF16)
        gh[part, 0, :, 256:384] = b[:, 128:256].astype(BF16)

    def send_back(part):
        ret_out[part] = acc_o[...].reshape(REL, CAP, LANES).astype(BF16)

        @pl.when(part == LAST)
        def _():
            ret_in[LAST, 0] = ret_out[LAST, 0]

        @pl.loop(first(part), REL)
        def _(j):
            give_back(part, j).start()

    def combine(part):
        @pl.loop(first(part), REL)
        def _(j):
            give_back(part, j).wait_recv()

        acc_t[...] += jnp.dot(
            pwt_s[part], ret_in[part].reshape(ROWS, LANES), preferred_element_type=F32
        )

    @pl.loop(0, PARTS + 7)
    def _(i):
        def when(part):
            return pl.when((part >= 0) & (part < PARTS))

        @when(i - 2)
        def _():
            arrived(x_copy, i - 2, 3)
            start(x_copy, i - 2, 4)

        @pl.when((i >= 1) & (i - 1 < BROAD))
        def _():
            arrived(x_copy, i - 1, 2)
            start(x_copy, i - 1, 3)

        for step in (2, 3, 4):
            @when(i - 2 - step)
            def _():
                arrived(h_copy, i - 2 - step, step - 1)
                start(h_copy, i - 2 - step, step)

        @when(i - 3)
        def _():
            for r in (0, 1, 7, 2, 6, 3, 5):
                x_dot(i - 3, r)
            arrived(x_copy, i - 3, 4)
            x_dot(i - 3, 4)
            activate(i - 3)
            start(h_copy, i - 3, 1)

        @pl.when(i == 0)
        def _():
            arrived(x_copy, 0, 1)

        @pl.when(i == 1)
        def _():
            @pl.loop(0, REL)
            def _(j):
                own_rows(1, j).wait_recv()
                for way in range(2):
                    side_rows(j, way).wait_recv()

        @pl.when((i >= 2) & (i < BROAD))
        def _():
            @pl.loop(0, REL)
            def _(j):
                near_rows(i, j).wait_recv()

        @pl.when(i < BROAD)
        def _():
            start(x_copy, i, 2)

        @pl.when((i >= BROAD) & (i < PARTS))
        def _():
            @pl.loop(first(i), REL)
            def _(j):
                wide_rows(i, j).wait_recv()

            start(x_copy, i, 3)

        @pl.when(i == 0)
        def _():
            prepare()

        @pl.when(i + AHEAD < BROAD)
        def _():
            send_part(i + AHEAD)

        @pl.when((i + AHEAD >= BROAD) & (i + AHEAD < PARTS))
        def _():
            send_wide(i + AHEAD)

        @when(i - 7)
        def _():
            for r in (0, 1, 7, 2, 6, 3, 5):
                h_dot(i - 7, r)
            arrived(h_copy, i - 7, 4)
            h_dot(i - 7, 4)
            send_back(i - 7)

        @when(i - 8)
        def _():
            left_here(h_copy, i - 8, (1, 2, 3, 4))

        @pl.when(i >= 9)
        def _():
            combine(i - 9)

            @pl.loop(0, REL)
            def _(j):
                give_back(i - 9, j).wait_send()

        @pl.when((i >= 4) & (i - 4 < BROAD))
        def _():
            left_here(x_copy, i - 4, (2,))

        @when(i - 4)
        def _():
            left_here(x_copy, i - 4, (3, 4))

        @pl.when(i == 0)
        def _():
            left_here(x_copy, 0, (1,))

        @pl.when(i < 2)
        def _():
            @pl.loop(0, REL)
            def _(j):
                own_rows(i, j).wait_send()

        @pl.when(i == 1)
        def _():
            @pl.loop(0, REL)
            def _(j):
                for way in range(2):
                    side_rows(j, way).wait_send()

        @pl.when((i >= 2) & (i < BROAD))
        def _():
            @pl.loop(0, REL)
            def _(j):
                near_rows(i, j).wait_send()

        @pl.when((i >= BROAD) & (i < PARTS))
        def _():
            @pl.loop(first(i), REL)
            def _(j):
                wide_rows(i, j).wait_send()

        @pl.when(i == 4)
        def _():
            for way in range(2):
                for step in (1, 2):
                    greet(step, way).wait_send()

            @pl.loop(1, NY)
            def _(n):
                stat_copy(n).wait()

            sums = stats_s[0]
            most = stats_s[0]
            for n in range(1, NY):
                sums = sums + stats_s[n]
                most = jnp.maximum(most, stats_s[n])
            peaks = most[1:2, :] * lax.rsqrt(sums[0:1, :] * (1.0 / D) + 1e-05)
            peaks_ref[...] = peaks.reshape(peaks_ref.shape)

    left_here(h_copy, LAST, (1, 2, 3, 4))
    combine(LAST - 1)
    combine(LAST)
    out_ref[...] = acc_t[...].T[0:FEAT, :].astype(BF16)

    for part in (LAST - 1, LAST):
        @pl.loop(first(part), REL)
        def _(j):
            give_back(part, j).wait_send()


def shards(hidden_in, norm_gain, expert_ids, route_weights, gate_weight, up_weight, down_weight):
    vmem = pl.BlockSpec(memory_space=pltpu.VMEM)
    dma = pltpu.SemaphoreType.DMA
    out, peaks = pl.pallas_call(
        kernel,
        out_shape=(
            jax.ShapeDtypeStruct((FEAT, TOK), BF16),
            jax.ShapeDtypeStruct((TOK,), F32),
        ),
        in_specs=[vmem] * 7,
        out_specs=(vmem, vmem),
        scratch_shapes=[
            pltpu.VMEM((5, LANES, TOK), BF16),
            pltpu.VMEM((NE, TOK), F32),
            pltpu.VMEM((NE, TOK), F32),
            pltpu.VMEM((PARTS, TOK, ROWS), BF16),
            pltpu.VMEM((PARTS, 5, REL, CAP, LANES), BF16),
            pltpu.VMEM((PARTS, NY, REL, CAP, LANES), BF16),
            pltpu.VMEM((PARTS, NY, HALF, LANES), BF16),
            pltpu.VMEM((NY, 2 * WIDE, LANES), BF16),
            pltpu.VMEM((NY, TALL, LANES), BF16),
            pltpu.VMEM((PARTS, REL, CAP, LANES), BF16),
            pltpu.VMEM((PARTS, REL, CAP, LANES), BF16),
            pltpu.VMEM((NY, 8, TOK), F32),
            pltpu.VMEM((ROWS, 2 * WIDE), F32),
            pltpu.VMEM((ROWS, LANES), F32),
            pltpu.VMEM((TOK, LANES), F32),
            dma((4,)),
            dma((4,)),
            dma((NE,)),
            dma((NE,)),
            dma((2 * REL,)),
            dma((2 * REL,)),
            dma((PARTS * 8,)),
            dma((PARTS * 8,)),
            dma((PARTS * 8,)),
            dma((PARTS * 8,)),
            dma((NE,)),
            dma((NE,)),
            dma((NY,)),
            dma((NY,)),
        ],
        compiler_params=pltpu.CompilerParams(
            collective_id=0, has_side_effects=True, vmem_limit_bytes=58 * 2**20
        ),
    )(
        hidden_in.T,
        norm_gain,
        expert_ids.T,
        route_weights.T,
        gate_weight[0],
        up_weight[0],
        down_weight[0],
    )
    return (out.T, peaks)


def solution(mesh):
    in_specs = (
        P("expert", "dp"),
        P("dp"),
        P("expert", None),
        P("expert", None),
        P("expert", "dp", None),
        P("expert", "dp", None),
        P("expert", None, "dp"),
    )
    out_specs = (P("expert", "dp"), P("expert"))
    return jax.shard_map(shards, mesh=mesh, in_specs=in_specs, out_specs=out_specs, check_vma=False)
```

```python
import jax
import jax.numpy as jnp
from jax import lax
from jax.experimental import pallas as pl
from jax.experimental.pallas import tpu as pltpu
from jax.sharding import PartitionSpec as P

D = 2880
TOP = 4
CAP = 24
MESH = pl.DeviceIdType.MESH
F32 = jnp.float32
BF16 = jnp.bfloat16

NY = 8
NX, NZ, NC = 4, 8, 2
NE = NX * NZ * NC
PARTS = NX * NC
LAST = PARTS - 1
BROAD = 6
REL = NZ
ROWS = REL * CAP
HALF = ROWS // 2
TOK = 256
FEAT = D // NY
UNITS = 180
LANES = 384
TAIL = 64
TALL = 320
SUM_ROW = 184
WIDE = 256
AHEAD = 4
OWN = 2
NT = (((1,), (1,)), ((), ()))


def kernel(
    hid_ref, gain_ref, ids_ref, rw_ref, gate_hbm, up_hbm, down_hbm,
    out_ref, peaks_ref,
    xs, key_s, wsel_s, pwt_s, send_s, gx, gh, wx_s, wd_s, ret_out, ret_in, stats_s,
    acc_x, acc_o, acc_t,
    pre_send, pre_recv, disp_send, disp_recv, side_send, side_recv, x_send_s, x_recv_s, h_send_s, h_recv_s,
    ret_send, ret_recv, st_send, st_recv, gate_ref, up_ref, down_ref, load_sem,
):
    my_y = lax.axis_index("dp")
    my_e = lax.axis_index("expert")
    my_x = my_e // (NZ * NC)
    my_z = (my_e // NC) % NZ
    my_c = my_e % NC
    right = (my_y + 1) % NY
    left = (my_y + NY - 1) % NY

    barrier = pltpu.get_barrier_semaphore()

    @pl.loop(1, NE)
    def _(i):
        pl.semaphore_signal(
            barrier, inc=1, device_id=(my_y, (my_e + i) % NE), device_id_type=MESH
        )

    @pl.loop(1, NY)
    def _(i):
        pl.semaphore_signal(
            barrier, inc=1, device_id=((my_y + i) % NY, my_e), device_id_type=MESH
        )

    def loads():
        pairs = ((gate_hbm, gate_ref), (up_hbm, up_ref), (down_hbm, down_ref))
        return [
            pltpu.make_async_copy(src, dst, load_sem.at[n]) for n, (src, dst) in enumerate(pairs)
        ]

    for load in loads():
        load.start()

    gain = jnp.broadcast_to(gain_ref[...].reshape(1, FEAT), (128, FEAT))
    gain = jnp.concatenate([gain, jnp.zeros((128, LANES - FEAT), F32)], axis=1).T[0:FEAT, :]
    hid = hid_ref[...].astype(F32)
    scaled = hid * jnp.concatenate([gain, gain], axis=1)
    total = jnp.sum(hid * hid, axis=0, keepdims=True)
    biggest = jnp.max(jnp.abs(scaled), axis=0, keepdims=True)
    high = total.astype(BF16).astype(F32)
    row = lax.broadcasted_iota(jnp.int32, (LANES - FEAT, TOK), 0)
    extra = jnp.where(row == 0, high, jnp.where(row == 1, total - high, 0.0))
    xs[OWN] = jnp.concatenate([scaled, extra], axis=0).astype(BF16)
    row8 = lax.broadcasted_iota(jnp.int32, (8, TOK), 0)
    stats_s[0] = jnp.where(row8 == 0, total, jnp.where(row8 == 1, biggest, 0.0))

    expert = lax.broadcasted_iota(jnp.int32, (NE, TOK), 0)
    named = jnp.zeros((NE, TOK), F32)
    weight = jnp.zeros((NE, TOK), F32)
    for j in range(TOP):
        hit = ids_ref[j : j + 1, :] == expert
        named = jnp.where(hit, 1.0, named)
        weight = jnp.where(hit, rw_ref[j : j + 1, :], weight)
    wsel_s[...] = weight
    earlier = (
        lax.broadcasted_iota(jnp.int32, (TOK, TOK), 0)
        < lax.broadcasted_iota(jnp.int32, (TOK, TOK), 1)
    )
    earlier = jnp.where(earlier, 1.0, 0.0).astype(BF16)
    before = jnp.dot(named.astype(BF16), earlier, preferred_element_type=F32)
    key_s[...] = jnp.where(named > 0.5, before, -1.0)

    def place(part, j, sign):
        turn = (part + 1) % PARTS
        dx, dc, dz = turn // NC, turn % NC, j
        x = (my_x + NX + sign * dx) % NX
        z = (my_z + NZ + sign * dz) % NZ
        c = (my_c + dc) % NC
        return (x * NZ + z) * NC + c

    rank = lax.broadcasted_iota(jnp.int32, (CAP, TOK), 0).astype(F32)

    def selection(part):
        picks, weighted = [], []
        for j in range(REL):
            e = place(part, j, 1)
            hit = key_s[pl.ds(e, 1), :] == rank
            picks.append(jnp.where(hit, 1.0, 0.0))
            weighted.append(jnp.where(hit, wsel_s[pl.ds(e, 1), :], 0.0))
        weighted = jnp.concatenate(weighted, axis=0)
        pwt_s[part] = weighted.T.astype(BF16)
        return jnp.concatenate(picks, axis=0).astype(BF16)

    def rows_of(pick, which):
        got = lax.dot_general(pick, xs[which], NT, preferred_element_type=F32)
        return got.reshape(REL, CAP, LANES).astype(BF16)

    def first(part):
        return jnp.where(part == LAST, 1, 0)

    def row_copy(part, j, slots, send, recv, sem):
        return pltpu.make_async_remote_copy(
            src_ref=send_s.at[part, slots, j],
            dst_ref=gx.at[part, slots, j],
            send_sem=send.at[sem],
            recv_sem=recv.at[sem],
            device_id=(my_y, place(part, j, 1)),
            device_id_type=MESH,
        )

    def own_rows(part, j):
        return row_copy(part, j, OWN, disp_send, disp_recv, part * REL + j)

    def near_rows(part, j):
        return row_copy(part, j, pl.ds(OWN - 1, 3), disp_send, disp_recv, part * REL + j)

    def wide_rows(part, j):
        return row_copy(part, j, pl.ds(0, 5), disp_send, disp_recv, part * REL + j)

    def side_rows(j, way):
        return row_copy(1, j, OWN - 1 + 2 * way, side_send, side_recv, way * REL + j)

    def slot(r):
        return (r + OWN) % NY

    def ring(buffer, sends, recvs, half, part, step, way, where):
        to = right if way == 0 else left
        if step < 4:
            r_from = step - 1 if way == 0 else (NY + 1 - step) % NY
            r_to = step if way == 0 else NY - step
            src = buffer.at[part, where(r_from)]
            dst = buffer.at[part, where(r_to)]
        else:
            r_from = 3 if way == 0 else 5
            rows = pl.ds(0 if way == 0 else half, half)
            src = buffer.at[part, where(r_from), rows]
            dst = buffer.at[part, where(4), rows]
        sem = part * 8 + way * 4 + step - 1
        return pltpu.make_async_remote_copy(
            src_ref=src,
            dst_ref=dst,
            send_sem=sends.at[sem],
            recv_sem=recvs.at[sem],
            device_id=(to, my_e),
            device_id_type=MESH,
        )

    def x_copy(part, step, way):
        return ring(gx, x_send_s, x_recv_s, REL // 2, part, step, way, slot)

    def h_copy(part, step, way):
        return ring(gh, h_send_s, h_recv_s, HALF // 2, part, step, way, lambda r: r)

    def start(copy, part, step):
        for way in range(2):
            copy(part, step, way).start()

    def arrived(copy, part, step):
        for way in range(2):
            copy(part, step, way).wait_recv()

    def left_here(copy, part, steps):
        for way in range(2):
            for step in steps:
                copy(part, step, way).wait_send()

    def give_back(part, j):
        return pltpu.make_async_remote_copy(
            src_ref=ret_out.at[part, j],
            dst_ref=ret_in.at[part, j],
            send_sem=ret_send.at[part * REL + j],
            recv_sem=ret_recv.at[part * REL + j],
            device_id=(my_y, place(part, j, -1)),
            device_id_type=MESH,
        )

    def greet(step, way):
        to, turn = (right, 1) if way == 0 else (left, -1)
        return pltpu.make_async_remote_copy(
            src_ref=xs.at[OWN + turn * (step - 1)],
            dst_ref=xs.at[OWN + turn * step],
            send_sem=pre_send.at[way * 2 + step - 1],
            recv_sem=pre_recv.at[way * 2 + step - 1],
            device_id=(to, my_e),
            device_id_type=MESH,
        )

    def stat_copy(i):
        return pltpu.make_async_remote_copy(
            src_ref=stats_s.at[0],
            dst_ref=stats_s.at[i],
            send_sem=st_send.at[i],
            recv_sem=st_recv.at[i],
            device_id=((my_y + i) % NY, my_e),
            device_id_type=MESH,
        )

    send_s[0, OWN] = rows_of(selection(0), OWN)
    second = selection(1)
    send_s[1, OWN] = rows_of(second, OWN)

    pl.semaphore_wait(barrier, NE - 1 + NY - 1)

    greet(1, 0).start()
    greet(1, 1).start()

    @pl.loop(0, 2)
    def _(part):
        @pl.loop(0, REL)
        def _(j):
            own_rows(part, j).start()

    @pl.loop(1, NY)
    def _(i):
        stat_copy(i).start()

    wx_s[...] = jnp.zeros_like(wx_s)
    for load in loads():
        load.wait()
    for k in range(NY):
        columns = slice(k * FEAT, (k + 1) * FEAT)
        wx_s[k, 0:UNITS, 0:FEAT] = gate_ref[:, columns]
        wx_s[k, WIDE : WIDE + UNITS, 0:FEAT] = up_ref[:, columns]

    @pl.loop(0, REL)
    def _(j):
        own_rows(0, j).wait_recv()

    start(x_copy, 0, 1)

    for way in range(2):
        greet(1, way).wait_recv()
        greet(2, way).start()

    for way in range(2):
        send_s[1, OWN - 1 + 2 * way] = rows_of(second, OWN - 1 + 2 * way)

        @pl.loop(0, REL)
        def _(j):
            side_rows(j, way).start()

    def send_part(part):
        picked = selection(part)
        for which in (OWN - 1, OWN, OWN + 1):
            send_s[part, which] = rows_of(picked, which)

        @pl.loop(0, REL)
        def _(j):
            near_rows(part, j).start()

    def send_wide(part):
        @pl.when(part == BROAD)
        def _():
            for way in range(2):
                greet(2, way).wait_recv()

        picked = selection(part)
        for which in range(5):
            send_s[part, which] = rows_of(picked, which)

        @pl.when(part == LAST)
        def _():
            for which in range(5):
                gx[LAST, which, 0] = send_s[LAST, which, 0]

        @pl.loop(first(part), REL)
        def _(j):
            wide_rows(part, j).start()

    @pl.loop(2, AHEAD)
    def _(part):
        send_part(part)

    def prepare():
        base = SUM_ROW - SUM_ROW % 16
        row16 = lax.broadcasted_iota(jnp.int32, (16, 128), 0) + base
        lane16 = lax.broadcasted_iota(jnp.int32, (16, 128), 1) + 256
        ones = (row16 == SUM_ROW) & ((lane16 == FEAT) | (lane16 == FEAT + 1))
        ones = jnp.where(ones, 1.0, 0.0).astype(BF16)
        for k in range(NY):
            wx_s[k, base : base + 16, 256:LANES] = wx_s[k, base : base + 16, 256:LANES] + ones
        wd_s[...] = jnp.zeros_like(wd_s)
        for k in range(NY):
            wd_s[k, TAIL : TAIL + UNITS, 0:FEAT] = down_ref[k * UNITS : (k + 1) * UNITS, :]
        acc_t[...] = jnp.zeros_like(acc_t)

    def x_dot(part, r):
        k = (my_y + NY - r) % NY
        block = gx[part, slot(r)].reshape(ROWS, LANES)
        add = lax.dot_general(block, wx_s[k], NT, preferred_element_type=F32)
        if r == 0:
            acc_x[...] = add
        else:
            acc_x[...] += add

    def h_dot(part, r):
        k = (my_y + NY - r) % NY
        for h in range(2):
            rows = slice(h * HALF, (h + 1) * HALF)
            cut = slice(TAIL, TALL) if h == 0 else slice(0, 256)
            lanes = slice(0, 256) if h == 0 else slice(128, 384)
            add = jnp.dot(gh[part, r, :, lanes], wd_s[k, cut, :], preferred_element_type=F32)
            if r == 0:
                acc_o[rows] = add
            else:
                acc_o[rows] += add

    def activate(part):
        g, u = acc_x[:, 0:WIDE], acc_x[:, WIDE : 2 * WIDE]
        inverse = lax.rsqrt(g[:, SUM_ROW : SUM_ROW + 1] * (1.0 / D) + 1e-05)
        g = g * inverse
        u = u * inverse
        hidden = g * jax.nn.sigmoid(1.702 * g) * (u + 1.0)
        a = hidden[0:HALF]
        b = pltpu.roll(hidden[HALF:ROWS], TAIL, 1)
        gh[part, 0, :, 0:128] = a[:, 0:128].astype(BF16)
        lane = lax.broadcasted_iota(jnp.int32, (HALF, 128), 1)
        middle = jnp.where(lane < TAIL, a[:, 128:256], b[:, 0:128])
        gh[part, 0, :, 128:256] = middle.astype(BF16)
        gh[part, 0, :, 256:384] = b[:, 128:256].astype(BF16)

    def send_back(part):
        ret_out[part] = acc_o[...].reshape(REL, CAP, LANES).astype(BF16)

        @pl.when(part == LAST)
        def _():
            ret_in[LAST, 0] = ret_out[LAST, 0]

        @pl.loop(first(part), REL)
        def _(j):
            give_back(part, j).start()

    def combine(part):
        @pl.loop(first(part), REL)
        def _(j):
            give_back(part, j).wait_recv()

        acc_t[...] += jnp.dot(
            pwt_s[part], ret_in[part].reshape(ROWS, LANES), preferred_element_type=F32
        )

    @pl.loop(0, PARTS + 7)
    def _(i):
        def when(part):
            return pl.when((part >= 0) & (part < PARTS))

        @when(i - 2)
        def _():
            arrived(x_copy, i - 2, 3)
            start(x_copy, i - 2, 4)

        @pl.when((i >= 1) & (i - 1 < BROAD))
        def _():
            arrived(x_copy, i - 1, 2)
            start(x_copy, i - 1, 3)

        for step in (2, 3, 4):
            @when(i - 2 - step)
            def _():
                arrived(h_copy, i - 2 - step, step - 1)
                start(h_copy, i - 2 - step, step)

        @when(i - 3)
        def _():
            for r in (0, 1, 7, 2, 6, 3, 5):
                x_dot(i - 3, r)
            arrived(x_copy, i - 3, 4)
            x_dot(i - 3, 4)
            activate(i - 3)
            start(h_copy, i - 3, 1)

        @pl.when(i == 0)
        def _():
            arrived(x_copy, 0, 1)

        @pl.when(i == 1)
        def _():
            @pl.loop(0, REL)
            def _(j):
                own_rows(1, j).wait_recv()
                for way in range(2):
                    side_rows(j, way).wait_recv()

        @pl.when((i >= 2) & (i < BROAD))
        def _():
            @pl.loop(0, REL)
            def _(j):
                near_rows(i, j).wait_recv()

        @pl.when(i < BROAD)
        def _():
            start(x_copy, i, 2)

        @pl.when((i >= BROAD) & (i < PARTS))
        def _():
            @pl.loop(first(i), REL)
            def _(j):
                wide_rows(i, j).wait_recv()

            start(x_copy, i, 3)

        @pl.when(i == 0)
        def _():
            prepare()

        @pl.when(i + AHEAD < BROAD)
        def _():
            send_part(i + AHEAD)

        @pl.when((i + AHEAD >= BROAD) & (i + AHEAD < PARTS))
        def _():
            send_wide(i + AHEAD)

        @when(i - 7)
        def _():
            for r in (0, 1, 7, 2, 6, 3, 5):
                h_dot(i - 7, r)
            arrived(h_copy, i - 7, 4)
            h_dot(i - 7, 4)
            send_back(i - 7)

        @when(i - 8)
        def _():
            left_here(h_copy, i - 8, (1, 2, 3, 4))

        @pl.when(i >= 9)
        def _():
            combine(i - 9)

            @pl.loop(0, REL)
            def _(j):
                give_back(i - 9, j).wait_send()

        @pl.when((i >= 4) & (i - 4 < BROAD))
        def _():
            left_here(x_copy, i - 4, (2,))

        @when(i - 4)
        def _():
            left_here(x_copy, i - 4, (3, 4))

        @pl.when(i == 0)
        def _():
            left_here(x_copy, 0, (1,))

        @pl.when(i < 2)
        def _():
            @pl.loop(0, REL)
            def _(j):
                own_rows(i, j).wait_send()

        @pl.when(i == 1)
        def _():
            @pl.loop(0, REL)
            def _(j):
                for way in range(2):
                    side_rows(j, way).wait_send()

        @pl.when((i >= 2) & (i < BROAD))
        def _():
            @pl.loop(0, REL)
            def _(j):
                near_rows(i, j).wait_send()

        @pl.when((i >= BROAD) & (i < PARTS))
        def _():
            @pl.loop(first(i), REL)
            def _(j):
                wide_rows(i, j).wait_send()

        @pl.when(i == 4)
        def _():
            for way in range(2):
                for step in (1, 2):
                    greet(step, way).wait_send()

            @pl.loop(1, NY)
            def _(n):
                stat_copy(n).wait()

            sums = stats_s[0]
            most = stats_s[0]
            for n in range(1, NY):
                sums = sums + stats_s[n]
                most = jnp.maximum(most, stats_s[n])
            peaks = most[1:2, :] * lax.rsqrt(sums[0:1, :] * (1.0 / D) + 1e-05)
            peaks_ref[...] = peaks.reshape(peaks_ref.shape)

    left_here(h_copy, LAST, (1, 2, 3, 4))
    combine(LAST - 1)
    combine(LAST)
    out_ref[...] = acc_t[...].T[0:FEAT, :].astype(BF16)

    for part in (LAST - 1, LAST):
        @pl.loop(first(part), REL)
        def _(j):
            give_back(part, j).wait_send()


def shards(hidden_in, norm_gain, expert_ids, route_weights, gate_weight, up_weight, down_weight):
    vmem = pl.BlockSpec(memory_space=pltpu.VMEM)
    dma = pltpu.SemaphoreType.DMA
    out, peaks = pl.pallas_call(
        kernel,
        out_shape=(
            jax.ShapeDtypeStruct((FEAT, TOK), BF16),
            jax.ShapeDtypeStruct((TOK,), F32),
        ),
        in_specs=[vmem] * 4 + [pl.BlockSpec(memory_space=pl.ANY)] * 3,
        out_specs=(vmem, vmem),
        scratch_shapes=[
            pltpu.VMEM((5, LANES, TOK), BF16),
            pltpu.VMEM((NE, TOK), F32),
            pltpu.VMEM((NE, TOK), F32),
            pltpu.VMEM((PARTS, TOK, ROWS), BF16),
            pltpu.VMEM((PARTS, 5, REL, CAP, LANES), BF16),
            pltpu.VMEM((PARTS, NY, REL, CAP, LANES), BF16),
            pltpu.VMEM((PARTS, NY, HALF, LANES), BF16),
            pltpu.VMEM((NY, 2 * WIDE, LANES), BF16),
            pltpu.VMEM((NY, TALL, LANES), BF16),
            pltpu.VMEM((PARTS, REL, CAP, LANES), BF16),
            pltpu.VMEM((PARTS, REL, CAP, LANES), BF16),
            pltpu.VMEM((NY, 8, TOK), F32),
            pltpu.VMEM((ROWS, 2 * WIDE), F32),
            pltpu.VMEM((ROWS, LANES), F32),
            pltpu.VMEM((TOK, LANES), F32),
            dma((4,)),
            dma((4,)),
            dma((NE,)),
            dma((NE,)),
            dma((2 * REL,)),
            dma((2 * REL,)),
            dma((PARTS * 8,)),
            dma((PARTS * 8,)),
            dma((PARTS * 8,)),
            dma((PARTS * 8,)),
            dma((NE,)),
            dma((NE,)),
            dma((NY,)),
            dma((NY,)),
            pltpu.VMEM((UNITS, D), BF16),
            pltpu.VMEM((UNITS, D), BF16),
            pltpu.VMEM((NY * UNITS, FEAT), BF16),
            dma((3,)),
        ],
        compiler_params=pltpu.CompilerParams(
            collective_id=0, has_side_effects=True, vmem_limit_bytes=58 * 2**20
        ),
    )(
        hidden_in.T,
        norm_gain,
        expert_ids.T,
        route_weights.T,
        gate_weight[0],
        up_weight[0],
        down_weight[0],
    )
    return (out.T, peaks)


def solution(mesh):
    in_specs = (
        P("expert", "dp"),
        P("dp"),
        P("expert", None),
        P("expert", None),
        P("expert", "dp", None),
        P("expert", "dp", None),
        P("expert", None, "dp"),
    )
    out_specs = (P("expert", "dp"), P("expert"))
    return jax.shard_map(shards, mesh=mesh, in_specs=in_specs, out_specs=out_specs, check_vma=False)
```
